32 devices in a mesh: seq: 8 (over y, x, core), chan: 4 (over z).
Axes of the slice: x: 2, y: 2, z: 4, core: 2. Of those that a mesh axis runs over, the one named last changes fastest.
Arguments:
- tokens: bfloat16 [6144, 4096], P('seq', 'chan'), may hold values from -4 to 4
- w_in: bfloat16 [8, 4096, 1296], P('chan', 'seq'), may hold values from -1 to 1
- conv_w: float32 [8, 4, 1280], P('chan'), may hold values from -3 to 3
- conv_b: float32 [8, 1280], P('chan'), may hold values from -3 to 3
- dt_bias: float32 [8, 16], P('chan'), may hold values from -8 to 2
- a_log: float32 [8, 16], P('chan'), may hold values from -4.6 to -3.7
- d_skip: float32 [8, 16], P('chan'), may hold values from 0.3 to 3
- norm_gain: float32 [8, 1024], P('chan'), may hold values from 0.5 to 1.5
Outputs:
- mixer_out: bfloat16 [6144, 8192], P('seq', 'chan')
The draws below stay inside these ranges and needn't reach their ends.
All inputs are finite; a program needn't handle non-finite values.
Results may differ from the reference program's by a relative error of at most 0.0076.
Values may be sent and summed in bfloat16 or wider, within the bound.
A program may use at most 128 MiB of HBM per device.

```python
import math
import jax
import jax.numpy as jnp
from jax import lax

D = 4096
P_SIZE = 64
N = 128
G = 8
KCONV = 4
Q = 128
HG = 16
GW = 1024
CW = 1280
COLS = 1296
TOKENS = 6144


def sign_pattern(key):
    flips = jax.random.bernoulli(jax.random.fold_in(key, 11), 0.5, (D,))
    return jnp.where(flips, 1.0, -1.0).astype(jnp.float32)


def draw_tokens(key, part):
    base_key = jax.random.fold_in(key, 21)
    drawn_vals = jnp.clip(jax.random.normal(base_key, (TOKENS, D), jnp.float32), -4.0, 4.0)
    spike_at = jax.random.randint(jax.random.fold_in(key, 22), (3,), 0, TOKENS)
    marked = jnp.any(jnp.arange(TOKENS)[:, None] == spike_at[None, :], axis=1)
    spiked = 2.7 * sign_pattern(key)[None, :] + 0.25 * drawn_vals
    return jnp.where(marked[:, None], spiked, drawn_vals).astype(jnp.bfloat16)


def draw_w_in(key, part):
    kernel_key = jax.random.fold_in(key, 31)
    drawn_vals = jnp.clip(jax.random.normal(kernel_key, (G, D, COLS), jnp.float32), -4.0, 4.0)
    drawn_vals = drawn_vals * D ** (-0.5)
    dt_mask = (jnp.arange(COLS) >= CW).astype(jnp.float32)
    extra = 9.0 / D * sign_pattern(key)[None, :, None] * dt_mask[None, None, :]
    return (drawn_vals + extra).astype(jnp.bfloat16)


def draw_dt_bias(key, part):
    fast_share = 0.5
    is_fast = jax.random.bernoulli(jax.random.fold_in(key, 41), fast_share, (G, HG))
    slow_vals = jax.random.uniform(jax.random.fold_in(key, 42), (G, HG), jnp.float32, -8.0, -7.0)
    fast_vals = jax.random.uniform(jax.random.fold_in(key, 43), (G, HG), jnp.float32, 1.0, 2.0)
    return jnp.where(is_fast, fast_vals, slow_vals)


def block_scale(stream_key, shape, pieces, low, top_value):
    def one(position, parts):
        steps = jax.random.uniform(jax.random.fold_in(jax.random.fold_in(stream_key, 6), position), (parts,), jnp.float32, low / len(pieces), top_value / len(pieces))
        return jnp.repeat(jnp.exp(steps), shape[position] // parts).reshape((-1,) + (1,) * (len(shape) - position - 1))

    level = one(*pieces[0])
    for cut in pieces[1:]:
        level = level * one(*cut)
    return level


def noise(own_key, extent, scale, reach, shards=(), held_as=jnp.bfloat16):
    result = scale * jax.random.normal(own_key, extent, jnp.float32)
    if shards:
        result = result * block_scale(own_key, extent, shards, -0.22, 0.18)
    return jnp.clip(result, -reach, reach).astype(held_as)


def setup_inputs(seed: int = 0) -> dict:
    key_of = jax.random.split(jax.random.key(seed), 9)
    return {
        "tokens": draw_tokens(jax.random.fold_in(key_of[8], 71), 0),
        "w_in": draw_w_in(jax.random.fold_in(key_of[8], 71), 0),
        "conv_w": noise(key_of[2], (G, KCONV, CW), 0.5, 3.0, ((0, 4),), jnp.float32),
        "conv_b": noise(key_of[3], (G, CW), 0.3, 3.0, ((0, 4),), jnp.float32),
        "dt_bias": draw_dt_bias(jax.random.fold_in(key_of[8], 71), 0),
        "a_log": jnp.clip(-4.6 + 0.89999986 * jax.random.uniform(key_of[5], (G, HG), jnp.float32) ** block_scale(key_of[5], (G, HG), ((0, 4),), -0.2, 0.2), -4.6, -3.7),
        "d_skip": jnp.clip(jnp.exp(math.log(3.0) - 2.3025851 * jax.random.uniform(key_of[6], (G, HG), jnp.float32) ** block_scale(key_of[6], (G, HG), ((0, 4),), -0.2, 0.2)), 0.3, 3.0),
        "norm_gain": jnp.clip(1.0 + 0.1 * jax.random.normal(key_of[7], (G, GW), jnp.float32), 0.5, 1.5),
    }


epsilon = 1e-05

def one_group(tokens, group_weight, group_kernel, group_shift, group_bias, group_alog, group_skip, group_gain):
    projected = jnp.dot(tokens, group_weight, preferred_element_type=jnp.float32)
    conv_in = projected[:, :CW].astype(jnp.bfloat16)
    raw_dt = projected[:, CW:]
    padded = jnp.concatenate([jnp.zeros((KCONV - 1, CW), jnp.bfloat16), conv_in], axis=0)
    pre_act = jnp.broadcast_to(group_shift[None, :], (TOKENS, CW))
    for offset in range(KCONV):
        pre_act = pre_act + group_kernel[offset][None, :] * padded[offset:offset + TOKENS]
    inputs = jax.nn.silu(pre_act).astype(jnp.bfloat16)
    block_count = TOKENS // Q
    x_all = inputs[:, :GW].reshape(block_count, Q, HG, P_SIZE)
    b_all = inputs[:, GW:GW + N].reshape(block_count, Q, N)
    c_all = inputs[:, GW + N:].reshape(block_count, Q, N)
    step_dt = jax.nn.softplus(raw_dt + group_bias[None, :]).reshape(block_count, Q, HG)
    decay_rate = -jnp.exp(group_alog)
    cumulative = jnp.cumsum(decay_rate[None, None, :] * step_dt, axis=1)
    causal = lax.broadcasted_iota(jnp.int32, (Q, Q), 0) >= lax.broadcasted_iota(jnp.int32, (Q, Q), 1)

    def per_block(state_now, block_in):
        x_blk, b_blk, c_blk, dt_blk, cum_blk = block_in
        scores = jnp.dot(c_blk, b_blk.T, preferred_element_type=jnp.float32)
        cum_cols = cum_blk.T
        dt_cols = dt_blk.T
        spread = cum_cols[:, :, None] - cum_cols[:, None, :]
        damping = jnp.where(causal[None], jnp.exp(jnp.minimum(spread, 0.0)), 0.0)
        weights = lax.optimization_barrier((scores[None] * damping * dt_cols[:, None, :]).astype(jnp.bfloat16)).astype(jnp.float32)
        inner = jnp.einsum('hij,jhp->ihp', weights, x_blk.astype(jnp.float32))
        rounded_state = lax.optimization_barrier(state_now.astype(jnp.bfloat16)).astype(jnp.float32)
        across = jnp.einsum('in,hpn->ihp', c_blk.astype(jnp.float32), rounded_state)
        activity = inner + jnp.exp(cum_blk)[:, :, None] * across + group_skip[None, :, None] * x_blk
        last_cum = cum_blk[-1]
        tail_factor = jnp.exp(last_cum[None, :] - cum_blk) * dt_blk
        scaled = lax.optimization_barrier((x_blk * tail_factor[:, :, None]).astype(jnp.bfloat16)).astype(jnp.float32)
        fresh_state = jnp.einsum('jhp,jn->hpn', scaled, b_blk.astype(jnp.float32))
        return (jnp.exp(last_cum)[:, None, None] * state_now + fresh_state, activity)
    zero_state = jnp.zeros((HG, P_SIZE, N), jnp.float32)
    _, activity = lax.scan(per_block, zero_state, (x_all, b_all, c_all, step_dt, cumulative))
    flat_act = activity.reshape(TOKENS, GW)
    inv_rms = lax.rsqrt(lax.optimization_barrier(jnp.mean(flat_act * flat_act, axis=-1, keepdims=True)) + epsilon)
    return (flat_act * inv_rms * group_gain[None, :]).astype(jnp.bfloat16)

def reference(tokens, w_in, conv_w, conv_b, dt_bias, a_log, d_skip, norm_gain):

    def group_entry(group_args):
        return one_group(tokens, group_args[0], group_args[1], group_args[2], group_args[3], group_args[4], group_args[5], group_args[6])
    outputs = lax.map(group_entry, (w_in, conv_w, conv_b, dt_bias, a_log, d_skip, norm_gain))
    return jnp.transpose(outputs, (1, 0, 2)).reshape(TOKENS, G * GW)
```

```python
import functools
import jax
import jax.numpy as jnp
from jax import lax
from jax.experimental import pallas as pl
from jax.experimental.pallas import tpu as pltpu
from jax.sharding import PartitionSpec as P

P_SIZE = 64
N = 128
KCONV = 4
Q = 128
HG = 16
GW = 1024
CW = 1280
RIM = 16
MESH = pl.DeviceIdType.MESH

epsilon = 1e-05


def project_kernel(
    lines, tok_ref, w_ref, conv_ref, dt_ref, rim_ref,
    tok_all, w_all, acc, own_sem, tok_send, tok_recv, w_own, w_fwd, w_sib, w_recv,
):
    s = lax.axis_index("seq")
    c = lax.axis_index("chan")
    groups, cols, depth = w_ref.shape
    rows, feats = tok_ref.shape
    half = rows // 2
    ratio = feats // depth
    core = s % 2
    sib = s + 1 - 2 * core
    xs = s + 2 - 4 * ((s // 2) % 2)
    ys = s + 4 - 8 * ((s // 4) % 2)
    diag = xs + ys - s
    fwd_shard = xs * (1 - core) + ys * core
    fwd_to = ys * (1 - core) + xs * core

    barrier = pltpu.get_barrier_semaphore()
    for other in (sib, xs, ys):
        pl.semaphore_signal(barrier, inc=1, device_id={"seq": other}, device_id_type=MESH)

    @pl.when(c > 0)
    def _():
        pl.semaphore_signal(barrier, inc=1, device_id={"chan": c - 1}, device_id_type=MESH)

    @pl.when(c < lines - 1)
    def _():
        pl.semaphore_signal(barrier, inc=1, device_id={"chan": c + 1}, device_id_type=MESH)

    pl.semaphore_wait(barrier, 3 + jnp.minimum(c, 1) + jnp.minimum(lines - 1 - c, 1))

    def tok_copy(shard, part, way, own):
        window = pl.ds(part * half, half)
        src = tok_ref.at[window] if own else tok_all.at[shard, window]
        return pltpu.make_async_remote_copy(
            src_ref=src,
            dst_ref=tok_all.at[shard, window],
            send_sem=tok_send.at[way, shard, part],
            recv_sem=tok_recv.at[shard, part],
            device_id={"chan": c + (1 if way else -1)},
            device_id_type=MESH,
        )

    def w_copy(shard, g, sem, to, own):
        src = w_ref.at[g] if own else w_all.at[shard, g]
        return pltpu.make_async_remote_copy(
            src_ref=src,
            dst_ref=w_all.at[shard, g],
            send_sem=sem,
            recv_sem=w_recv.at[shard, g],
            device_id={"seq": to},
            device_id_type=MESH,
        )

    def tok_sends(k, part, act):
        @pl.when((c - k >= 0) & (c < lines - 1))
        def _():
            act(tok_copy(c - k, part, 1, k == 0))

        @pl.when((c + k < lines) & (c > 0))
        def _():
            act(tok_copy(c + k, part, 0, k == 0))

    def tok_arrive(k, part):
        @pl.when(c - k >= 0)
        def _():
            tok_copy(c - k, part, 1, False).wait_recv()

        @pl.when(c + k < lines)
        def _():
            tok_copy(c + k, part, 0, False).wait_recv()

    def start(copy):
        copy.start()

    def sent(copy):
        copy.wait_send()

    own_tok = pltpu.make_async_copy(tok_ref, tok_all.at[c], own_sem.at[0])
    own_w = pltpu.make_async_copy(w_ref, w_all.at[s], own_sem.at[1])
    for part in range(2):
        tok_sends(0, part, start)
        for i, to in enumerate((xs, ys, sib)):
            w_copy(s, part, w_own.at[i, part], to, True).start()
    own_tok.start()
    own_w.start()

    def near_weights(g):
        w_copy(xs, g, w_sib.at[0, g], sib, False).wait_recv()
        w_copy(ys, g, w_sib.at[1, g], sib, False).wait_recv()
        w_copy(fwd_shard, g, w_fwd.at[g], fwd_to, False).start()
        w_copy(xs, g, w_sib.at[0, g], sib, False).start()
        w_copy(ys, g, w_sib.at[1, g], sib, False).start()

    def far_weights(g):
        w_copy(diag, g, w_sib.at[2, g], sib, False).wait_recv()
        w_copy(diag, g, w_sib.at[2, g], sib, False).start()

    def relay(k, part):
        tok_arrive(k, part)
        if k < lines - 1:
            tok_sends(k, part, start)

    relay(1, 0)
    near_weights(0)
    relay(1, 1)
    if lines > 2:
        relay(2, 0)
    near_weights(1)
    if lines > 2:
        relay(2, 1)
    far_weights(0)
    far_weights(1)
    for k in range(3, lines - 1):
        relay(k, 0)
        relay(k, 1)
    for shard in (sib, sib + xs - s, sib + ys - s, sib + diag - s):
        for g in range(groups):
            w_copy(shard, g, w_own.at[2, g], sib, False).wait_recv()
    own_tok.wait()
    own_w.wait()

    tiles = 3
    tall = cols // tiles

    def product(shard, first):
        @pl.loop(0, groups * tiles)
        def _(step):
            g = step // tiles
            window = pl.ds(pl.multiple_of((step % tiles) * tall, 16), tall)
            total = None
            for i in range(ratio):
                term = lax.dot_general(
                    w_all[shard * ratio + i, g, window, :],
                    tok_all[shard, :, i * depth : (i + 1) * depth],
                    (((1,), (1,)), ((), ())),
                    preferred_element_type=jnp.float32,
                )
                total = term if total is None else total + term
            if first:
                acc[g, window, :] = total
            else:
                acc[g, window, :] += total

    product(c, True)
    for k in range(1, lines):
        if k >= 3 and k == lines - 1:
            tok_arrive(k, 0)
            tok_arrive(k, 1)

        @pl.when(c - k >= 0)
        def _():
            product(c - k, False)

        @pl.when(c + k < lines)
        def _():
            product(c + k, False)

    for g in range(groups):
        conv_ref[g] = acc[g, :CW, :].astype(jnp.bfloat16)
        dt_ref[g] = acc[g, CW:, :]
        rim_ref[g] = acc[g, :CW, rows - Q :].T[Q - RIM :].astype(jnp.bfloat16)

    for part in range(2):
        for k in range(lines - 1):
            tok_sends(k, part, sent)
        for i, to in enumerate((xs, ys, sib)):
            w_copy(s, part, w_own.at[i, part], to, True).wait_send()
        w_copy(fwd_shard, part, w_fwd.at[part], fwd_to, False).wait_send()
        w_copy(xs, part, w_sib.at[0, part], sib, False).wait_send()
        w_copy(ys, part, w_sib.at[1, part], sib, False).wait_send()
        w_copy(diag, part, w_sib.at[2, part], sib, False).wait_send()


def project(tokens, w_turned, lines, ranks):
    groups, cols, depth = w_turned.shape
    rows, feats = tokens.shape
    shapes = (
        jax.ShapeDtypeStruct((groups, CW, rows), jnp.bfloat16),
        jax.ShapeDtypeStruct((groups, cols - CW, rows), jnp.float32),
        jax.ShapeDtypeStruct((groups, RIM, CW), jnp.bfloat16),
    )
    if ranks == 8 and groups == 2 and lines > 1:
        dma = pltpu.SemaphoreType.DMA
        return pl.pallas_call(
            functools.partial(project_kernel, lines),
            out_shape=shapes,
            in_specs=[pl.BlockSpec(memory_space=pl.ANY)] * 2,
            out_specs=(pl.BlockSpec(memory_space=pltpu.VMEM),) * 3,
            scratch_shapes=[
                pltpu.VMEM((lines, rows, feats), jnp.bfloat16),
                pltpu.VMEM((ranks, groups, cols, depth), jnp.bfloat16),
                pltpu.VMEM((groups, cols, rows), jnp.float32),
                dma((2,)),
                dma((2, lines, 2)),
                dma((lines, 2)),
                dma((3, 2)),
                dma((2,)),
                dma((3, 2)),
                dma((ranks, 2)),
            ],
            compiler_params=pltpu.CompilerParams(
                collective_id=0, has_side_effects=True, vmem_limit_bytes=56 * 2**20
            ),
        )(tokens, w_turned)
    gathered = lax.all_gather(tokens, "chan", axis=1, tiled=True)
    whole = lax.all_gather(w_turned, "seq", axis=2, tiled=True)
    turned = jnp.einsum("gcd,td->gct", whole, gathered, preferred_element_type=jnp.float32)
    conv = turned[:, :CW].astype(jnp.bfloat16)
    return conv, turned[:, CW:], jnp.swapaxes(conv[:, :, rows - RIM :], 1, 2)


def shifted(block, axis, distance):
    devices = range(lax.axis_size(axis))
    route = [(i - distance, i) for i in devices if i - distance in devices]
    return lax.ppermute(block, axis, route)


def entering(part, axis, combine, identity):
    place = lax.axis_index(axis)
    gathered = jax.tree.map(lambda a: lax.all_gather(a, axis), part)
    state = jax.tree.map(lambda a, e: jnp.zeros_like(a) + jnp.asarray(e, a.dtype), part, identity)

    def one(step, state):
        return combine(
            state, jax.tree.map(lambda a: lax.dynamic_index_in_dim(a, step, 0, False), gathered)
        )

    return lax.fori_loop(0, place, one, state)


def combine_states(earlier, later_one):
    return (earlier[0] * later_one[0], later_one[0][..., None, None] * earlier[1] + later_one[1])


def mix_groups(tokens, w_in, conv_w, conv_b, dt_bias, a_log, d_skip, norm_gain):
    groups = w_in.shape[0]
    row_count = tokens.shape[0]
    conv_turned, dt_turned, rim = project(
        tokens, jnp.swapaxes(w_in, 1, 2), lax.axis_size("chan"), lax.axis_size("seq")
    )
    conv_in = jnp.transpose(conv_turned, (2, 0, 1))
    raw_dt = jnp.transpose(dt_turned, (2, 0, 1))
    rim_rows = jnp.swapaxes(shifted(rim, "seq", 1)[:, RIM - (KCONV - 1) :], 0, 1)
    padded = jnp.concatenate([rim_rows, conv_in], axis=0)
    pre_act = jnp.broadcast_to(conv_b[None], (row_count, groups, CW))
    for offset in range(KCONV):
        pre_act = pre_act + conv_w[None, :, offset] * padded[offset : offset + row_count]
    inputs = jax.nn.silu(pre_act).astype(jnp.bfloat16)
    block_count = row_count // Q
    blocked = inputs.reshape(block_count, Q, groups, CW)
    x_all = blocked[..., :GW].reshape(block_count, Q, groups, HG, P_SIZE)
    b_all = blocked[..., GW : GW + N]
    c_all = blocked[..., GW + N :]
    step_dt = jax.nn.softplus(raw_dt + dt_bias[None]).reshape(block_count, Q, groups, HG)
    decay_rate = -jnp.exp(a_log)
    cumulative = jnp.cumsum(decay_rate[None, None] * step_dt, axis=1)
    causal = lax.broadcasted_iota(jnp.int32, (Q, Q), 0) >= lax.broadcasted_iota(
        jnp.int32, (Q, Q), 1
    )

    def local_block(carried, block_in):
        state_now, factor = carried
        x_blk, b_blk, c_blk, dt_blk, cum_blk = block_in
        scores = jnp.einsum("ign,jgn->gij", c_blk, b_blk, preferred_element_type=jnp.float32)
        cum_cols = jnp.transpose(cum_blk, (1, 2, 0))
        dt_cols = jnp.transpose(dt_blk, (1, 2, 0))
        spread = cum_cols[..., :, None] - cum_cols[..., None, :]
        damping = jnp.where(causal, jnp.exp(jnp.minimum(spread, 0.0)), 0.0)
        weights = (scores[:, None] * damping * dt_cols[..., None, :]).astype(jnp.bfloat16)
        partial_y = jnp.einsum(
            "ghij,jghp->ighp", weights, x_blk, preferred_element_type=jnp.float32
        )
        partial_y = partial_y + d_skip[None, :, :, None] * x_blk
        last_cum = cum_blk[-1]
        tail_factor = jnp.exp(last_cum[None] - cum_blk) * dt_blk
        scaled = (x_blk * tail_factor[..., None]).astype(jnp.bfloat16)
        fresh_state = jnp.einsum(
            "jghp,jgn->ghpn", scaled, b_blk, preferred_element_type=jnp.float32
        )
        keep_blk = jnp.exp(last_cum)
        carried_next = (keep_blk[..., None, None] * state_now + fresh_state, factor * keep_blk)
        return (carried_next, (partial_y, fresh_state, keep_blk))

    zero_state = jnp.zeros((groups, HG, P_SIZE, N), jnp.float32)
    unit_keep = jnp.ones((groups, HG), jnp.float32)
    (local_end, local_keep), (partial_all, fresh_all, keep_all) = lax.scan(
        local_block, (zero_state, unit_keep), (x_all, b_all, c_all, step_dt, cumulative)
    )
    _, incoming = entering((local_keep, local_end), "seq", combine_states, (unit_keep, zero_state))

    def finish_block(state_now, block_in):
        partial_y, fresh_state, keep_blk, c_blk, cum_blk = block_in
        across = jnp.einsum(
            "ign,ghpn->ighp",
            c_blk,
            state_now.astype(jnp.bfloat16),
            preferred_element_type=jnp.float32,
        )
        activity = partial_y + jnp.exp(cum_blk)[..., None] * across
        flat_act = activity.reshape(Q, groups, GW)
        inv_rms = lax.rsqrt(jnp.mean(flat_act * flat_act, axis=-1, keepdims=True) + epsilon)
        normed = (flat_act * inv_rms * norm_gain[None]).astype(jnp.bfloat16)
        return (keep_blk[..., None, None] * state_now + fresh_state, normed)

    _, outputs = lax.scan(
        finish_block, incoming, (partial_all, fresh_all, keep_all, c_all, cumulative)
    )
    return outputs.reshape(row_count, groups * GW)


def per_device(tokens, w_in, conv_w, conv_b, dt_bias, a_log, d_skip, norm_gain):
    return mix_groups(tokens, w_in, conv_w, conv_b, dt_bias, a_log, d_skip, norm_gain)


def solution(mesh):
    return jax.shard_map(
        per_device,
        mesh=mesh,
        in_specs=(
            P("seq", "chan"),
            P("chan", "seq", None),
            P("chan", None, None),
            P("chan", None),
            P("chan", None),
            P("chan", None),
            P("chan", None),
            P("chan", None),
        ),
        out_specs=P("seq", "chan"),
        check_vma=False,
    )
```

```python
import functools
import jax
import jax.numpy as jnp
from jax import lax
from jax.experimental import pallas as pl
from jax.experimental.pallas import tpu as pltpu
from jax.sharding import PartitionSpec as P

P_SIZE = 64
N = 128
KCONV = 4
Q = 128
HG = 16
GW = 1024
CW = 1280
RIM = 16
MESH = pl.DeviceIdType.MESH

epsilon = 1e-05


def project_kernel(
    lines, tok_ref, w_ref, conv_ref, dt_ref, rim_ref,
    tok_all, w_all, acc, own_sem, tok_send, tok_recv, w_own, w_fwd, w_sib, w_recv,
):
    s = lax.axis_index("seq")
    c = lax.axis_index("chan")
    groups, cols, depth = w_ref.shape
    rows, feats = tok_ref.shape
    half = rows // 2
    ratio = feats // depth
    core = s % 2
    sib = s + 1 - 2 * core
    xs = s + 2 - 4 * ((s // 2) % 2)
    ys = s + 4 - 8 * ((s // 4) % 2)
    diag = xs + ys - s
    fwd_shard = xs * (1 - core) + ys * core
    fwd_to = ys * (1 - core) + xs * core

    barrier = pltpu.get_barrier_semaphore()
    for other in (sib, xs, ys):
        pl.semaphore_signal(barrier, inc=1, device_id={"seq": other}, device_id_type=MESH)

    @pl.when(c > 0)
    def _():
        pl.semaphore_signal(barrier, inc=1, device_id={"chan": c - 1}, device_id_type=MESH)

    @pl.when(c < lines - 1)
    def _():
        pl.semaphore_signal(barrier, inc=1, device_id={"chan": c + 1}, device_id_type=MESH)

    pl.semaphore_wait(barrier, 3 + jnp.minimum(c, 1) + jnp.minimum(lines - 1 - c, 1))

    def tok_copy(shard, part, way, own):
        window = pl.ds(part * half, half)
        src = tok_ref.at[window] if own else tok_all.at[shard, window]
        return pltpu.make_async_remote_copy(
            src_ref=src,
            dst_ref=tok_all.at[shard, window],
            send_sem=tok_send.at[way, shard, part],
            recv_sem=tok_recv.at[shard, part],
            device_id={"chan": c + (1 if way else -1)},
            device_id_type=MESH,
        )

    def w_copy(shard, g, sem, to, own):
        src = w_ref.at[g] if own else w_all.at[shard, g]
        return pltpu.make_async_remote_copy(
            src_ref=src,
            dst_ref=w_all.at[shard, g],
            send_sem=sem,
            recv_sem=w_recv.at[shard, g],
            device_id={"seq": to},
            device_id_type=MESH,
        )

    def tok_sends(k, part, act):
        @pl.when((c - k >= 0) & (c < lines - 1))
        def _():
            act(tok_copy(c - k, part, 1, k == 0))

        @pl.when((c + k < lines) & (c > 0))
        def _():
            act(tok_copy(c + k, part, 0, k == 0))

    def tok_arrive(k, part):
        @pl.when(c - k >= 0)
        def _():
            tok_copy(c - k, part, 1, False).wait_recv()

        @pl.when(c + k < lines)
        def _():
            tok_copy(c + k, part, 0, False).wait_recv()

    def start(copy):
        copy.start()

    def sent(copy):
        copy.wait_send()

    own_tok = pltpu.make_async_copy(tok_ref, tok_all.at[c], own_sem.at[0])
    own_w = pltpu.make_async_copy(w_ref, w_all.at[s], own_sem.at[1])
    for part in range(2):
        tok_sends(0, part, start)
        for i, to in enumerate((xs, ys, sib)):
            w_copy(s, part, w_own.at[i, part], to, True).start()
    own_tok.start()
    own_w.start()

    def near_weights(g):
        w_copy(xs, g, w_sib.at[0, g], sib, False).wait_recv()
        w_copy(ys, g, w_sib.at[1, g], sib, False).wait_recv()
        w_copy(fwd_shard, g, w_fwd.at[g], fwd_to, False).start()
        w_copy(xs, g, w_sib.at[0, g], sib, False).start()
        w_copy(ys, g, w_sib.at[1, g], sib, False).start()

    def far_weights(g):
        w_copy(diag, g, w_sib.at[2, g], sib, False).wait_recv()
        w_copy(diag, g, w_sib.at[2, g], sib, False).start()

    def relay(k, part):
        tok_arrive(k, part)
        if k < lines - 1:
            tok_sends(k, part, start)

    relay(1, 0)
    near_weights(0)
    relay(1, 1)
    if lines > 2:
        relay(2, 0)
    near_weights(1)
    if lines > 2:
        relay(2, 1)
    far_weights(0)
    far_weights(1)
    for k in range(3, lines - 1):
        relay(k, 0)
        relay(k, 1)
    for shard in (sib, sib + xs - s, sib + ys - s, sib + diag - s):
        for g in range(groups):
            w_copy(shard, g, w_own.at[2, g], sib, False).wait_recv()
    own_tok.wait()
    own_w.wait()

    tiles = 3
    tall = cols // tiles

    def product(shard, first):
        @pl.loop(0, groups * tiles)
        def _(step):
            g = step // tiles
            window = pl.ds(pl.multiple_of((step % tiles) * tall, 16), tall)
            total = None
            for i in range(ratio):
                term = lax.dot_general(
                    w_all[shard * ratio + i, g, window, :],
                    tok_all[shard, :, i * depth : (i + 1) * depth],
                    (((1,), (1,)), ((), ())),
                    preferred_element_type=jnp.float32,
                )
                total = term if total is None else total + term
            if first:
                acc[g, window, :] = total
            else:
                acc[g, window, :] += total

    product(c, True)
    for k in range(1, lines):
        if k >= 3 and k == lines - 1:
            tok_arrive(k, 0)
            tok_arrive(k, 1)

        @pl.when(c - k >= 0)
        def _():
            product(c - k, False)

        @pl.when(c + k < lines)
        def _():
            product(c + k, False)

    for g in range(groups):
        conv_ref[g] = acc[g, :CW, :].astype(jnp.bfloat16)
        dt_ref[g] = acc[g, CW:, :]
        rim_ref[g] = acc[g, :CW, rows - Q :].T[Q - RIM :].astype(jnp.bfloat16)

    for part in range(2):
        for k in range(lines - 1):
            tok_sends(k, part, sent)
        for i, to in enumerate((xs, ys, sib)):
            w_copy(s, part, w_own.at[i, part], to, True).wait_send()
        w_copy(fwd_shard, part, w_fwd.at[part], fwd_to, False).wait_send()
        w_copy(xs, part, w_sib.at[0, part], sib, False).wait_send()
        w_copy(ys, part, w_sib.at[1, part], sib, False).wait_send()
        w_copy(diag, part, w_sib.at[2, part], sib, False).wait_send()


def project(tokens, w_turned, lines, ranks):
    groups, cols, depth = w_turned.shape
    rows, feats = tokens.shape
    shapes = (
        jax.ShapeDtypeStruct((groups, CW, rows), jnp.bfloat16),
        jax.ShapeDtypeStruct((groups, cols - CW, rows), jnp.float32),
        jax.ShapeDtypeStruct((groups, RIM, CW), jnp.bfloat16),
    )
    if ranks == 8 and groups == 2 and lines > 1:
        dma = pltpu.SemaphoreType.DMA
        return pl.pallas_call(
            functools.partial(project_kernel, lines),
            out_shape=shapes,
            in_specs=[pl.BlockSpec(memory_space=pl.ANY)] * 2,
            out_specs=(pl.BlockSpec(memory_space=pltpu.VMEM),) * 3,
            scratch_shapes=[
                pltpu.VMEM((lines, rows, feats), jnp.bfloat16),
                pltpu.VMEM((ranks, groups, cols, depth), jnp.bfloat16),
                pltpu.VMEM((groups, cols, rows), jnp.float32),
                dma((2,)),
                dma((2, lines, 2)),
                dma((lines, 2)),
                dma((3, 2)),
                dma((2,)),
                dma((3, 2)),
                dma((ranks, 2)),
            ],
            compiler_params=pltpu.CompilerParams(
                collective_id=0, has_side_effects=True, vmem_limit_bytes=56 * 2**20
            ),
        )(tokens, w_turned)
    gathered = lax.all_gather(tokens, "chan", axis=1, tiled=True)
    whole = lax.all_gather(w_turned, "seq", axis=2, tiled=True)
    turned = jnp.einsum("gcd,td->gct", whole, gathered, preferred_element_type=jnp.float32)
    conv = turned[:, :CW].astype(jnp.bfloat16)
    return conv, turned[:, CW:], jnp.swapaxes(conv[:, :, rows - RIM :], 1, 2)


def mix_kernel(
    ranks, conv_ref, dt_ref, rim_ref, par_ref, head_ref, skip_ref,
    part_ref, c_ref, dec_ref, in_ref,
    act, rim_t, dts, cums, states, total, keep, before, keep_before,
    out_state, out_keep, got_state, got_keep, send_sem, recv_sem,
):
    s = lax.axis_index("seq")
    groups, _, rows = conv_ref.shape
    blocks = rows // Q
    steps = ranks.bit_length() - 1
    partners = [s + 2**i - 2 ** (i + 1) * ((s // 2**i) % 2) for i in range(steps)]

    barrier = pltpu.get_barrier_semaphore()
    for other in partners:
        pl.semaphore_signal(barrier, inc=1, device_id={"seq": other}, device_id_type=MESH)
    pl.semaphore_wait(barrier, steps)

    lane = lax.broadcasted_iota(jnp.int32, (32, Q), 1)
    for g in range(groups):
        turned = jnp.concatenate(
            [jnp.zeros((Q - RIM, CW), jnp.float32), rim_ref[g].astype(jnp.float32)], axis=0
        )
        rim_t[g] = turned.T

    strips = CW // 32

    @pl.loop(0, groups * strips)
    def _(step):
        g = step // strips
        window = pl.ds(pl.multiple_of((step % strips) * 32, 32), 32)
        par = par_ref[g, window, :]
        taps = [jnp.broadcast_to(par[:, k : k + 1], (32, Q)) for k in range(KCONV + 1)]
        earlier = rim_t[g, window, :]
        old = [pltpu.roll(earlier, d, 1) for d in range(1, KCONV)]
        for q in range(blocks):
            now = conv_ref[g, window, q * Q : (q + 1) * Q].astype(jnp.float32)
            pre = taps[KCONV] + taps[KCONV - 1] * now
            fresh = [pltpu.roll(now, d, 1) for d in range(1, KCONV)]
            for d in range(1, KCONV):
                pre = pre + taps[KCONV - 1 - d] * jnp.where(lane < d, old[d - 1], fresh[d - 1])
            old = fresh
            value = 0.5 * pre * (1.0 + jnp.tanh(0.5 * pre))
            act[g, window, q * Q : (q + 1) * Q] = value.astype(jnp.bfloat16)

    row = lax.broadcasted_iota(jnp.int32, (Q, Q), 0)
    col = lax.broadcasted_iota(jnp.int32, (Q, Q), 1)
    causal = row <= col
    upper = jnp.where(causal, 1.0, 0.0)
    for g in range(groups):
        c_ref[g] = act[g, GW + N :, :]
        heads = head_ref[g]
        raw = dt_ref[g] + heads[:, 0:1]
        step_dt = jnp.maximum(raw, 0.0) + jnp.log1p(jnp.exp(-jnp.abs(raw)))
        dts[g] = step_dt
        slope = -jnp.exp(heads[:, 1:2]) * step_dt
        base = jnp.zeros((HG, 1), jnp.float32)
        for q in range(blocks):
            tile = slice(q * Q, (q + 1) * Q)
            cum = jnp.dot(
                slope[:, tile], upper,
                precision=lax.Precision.HIGHEST, preferred_element_type=jnp.float32,
            )
            cums[g, :, tile] = cum
            dec_ref[g, :, tile] = jnp.exp(cum + base)
            base = base + cum[:, Q - 1 :]
        keep[g] = jnp.broadcast_to(jnp.exp(base), (HG, Q))
        total[g] = jnp.zeros((GW, N), jnp.float32)

    @pl.loop(0, groups * blocks)
    def _(unit):
        g, q = unit // blocks, unit % blocks
        tile = pl.ds(pl.multiple_of(q * Q, Q), Q)
        cum = cums[g, :, tile]
        last = cum[:, Q - 1 :]
        tail = jnp.exp(last - cum) * dts[g, :, tile]
        held = jnp.broadcast_to(jnp.exp(last), (HG, Q))
        states[g, q] = total[g].astype(jnp.bfloat16)
        b = act[g, GW : GW + N, tile].astype(jnp.float32).T.astype(jnp.bfloat16)
        for h in range(0, HG, 4):
            x = act[g, h * P_SIZE : (h + 4) * P_SIZE, tile].astype(jnp.float32)
            scaled = x.reshape(4, P_SIZE, Q) * tail[h : h + 4][:, None, :]
            scaled = scaled.reshape(4 * P_SIZE, Q).astype(jnp.bfloat16)
            fresh = jnp.dot(scaled, b, preferred_element_type=jnp.float32)
            for i in range(4):
                span = slice((h + i) * P_SIZE, (h + i + 1) * P_SIZE)
                total[g, span, :] = (
                    held[h + i : h + i + 1] * total[g, span, :]
                    + fresh[i * P_SIZE : (i + 1) * P_SIZE]
                )

    def inner(unit):
        g, q = unit // blocks, unit % blocks
        tile = pl.ds(pl.multiple_of(q * Q, Q), Q)
        cum = cums[g, :, tile]
        tall = jnp.concatenate([cum, jnp.zeros((Q - HG, Q), jnp.float32)], axis=0).T
        dt = dts[g, :, tile]
        grown = jnp.exp(cum)
        b = act[g, GW : GW + N, tile].astype(jnp.float32).T.astype(jnp.bfloat16)
        c = act[g, GW + N :, tile]
        scores = jnp.where(causal, jnp.dot(b, c, preferred_element_type=jnp.float32), 0.0)
        for h in range(HG):
            span = slice(h * P_SIZE, (h + 1) * P_SIZE)
            x = act[g, span, tile].astype(jnp.float32)
            across = jnp.dot(states[g, q, span, :], c, preferred_element_type=jnp.float32)
            spread = cum[h : h + 1] - tall[:, h : h + 1]
            weights = (scores * jnp.exp(jnp.minimum(spread, 0.0))).astype(jnp.bfloat16)
            stepped = (x * dt[h : h + 1]).astype(jnp.bfloat16)
            y = jnp.dot(stepped, weights, preferred_element_type=jnp.float32)
            part_ref[g, span, tile] = y + grown[h : h + 1] * across + skip_ref[g, h] * x

    def exchange(i):
        return [
            pltpu.make_async_remote_copy(
                src_ref=src.at[i], dst_ref=dst.at[i],
                send_sem=send_sem.at[i, j], recv_sem=recv_sem.at[i, j],
                device_id={"seq": partners[i]}, device_id_type=MESH,
            )
            for j, (src, dst) in enumerate(((out_state, got_state), (out_keep, got_keep)))
        ]

    def send(i):
        out_state[i] = total[...].astype(jnp.bfloat16)
        out_keep[i] = keep[...]
        for copy in exchange(i):
            copy.start()

    before[...] = jnp.zeros_like(before)
    keep_before[...] = jnp.ones_like(keep_before)
    units = groups * blocks
    for i in range(steps):
        send(i)
        pl.loop(units * i // steps, units * (i + 1) // steps)(inner)
        for copy in exchange(i):
            copy.wait_recv()
        upper_half = (s // 2**i) % 2

        @pl.when(upper_half == 1)
        def _():
            for g in range(groups):
                for h in range(HG):
                    span = slice(h * P_SIZE, (h + 1) * P_SIZE)
                    got = got_state[i, g, span, :].astype(jnp.float32)
                    before[g, span, :] += keep_before[g, h : h + 1] * got
                    if i < steps - 1:
                        total[g, span, :] += keep[g, h : h + 1] * got
            keep_before[...] = keep_before[...] * got_keep[i]

        if i < steps - 1:

            @pl.when(upper_half == 0)
            def _():
                for g in range(groups):
                    for h in range(HG):
                        span = slice(h * P_SIZE, (h + 1) * P_SIZE)
                        got = got_state[i, g, span, :].astype(jnp.float32)
                        total[g, span, :] = got_keep[i, g, h : h + 1] * total[g, span, :] + got

            keep[...] = keep[...] * got_keep[i]

    in_ref[...] = before[...].astype(jnp.bfloat16)
    for i in range(steps):
        for copy in exchange(i):
            copy.wait_send()


def mix(conv, dt, rim, par, heads, skip, ranks):
    groups, _, rows = conv.shape
    blocks = rows // Q
    steps = ranks.bit_length() - 1
    vmem = pl.BlockSpec(memory_space=pltpu.VMEM)
    f32, bf16 = jnp.float32, jnp.bfloat16
    return pl.pallas_call(
        functools.partial(mix_kernel, ranks),
        out_shape=(
            jax.ShapeDtypeStruct((groups, GW, rows), f32),
            jax.ShapeDtypeStruct((groups, N, rows), bf16),
            jax.ShapeDtypeStruct((groups, HG, rows), f32),
            jax.ShapeDtypeStruct((groups, GW, N), bf16),
        ),
        in_specs=[vmem] * 5 + [pl.BlockSpec(memory_space=pltpu.SMEM)],
        out_specs=(vmem,) * 4,
        scratch_shapes=[
            pltpu.VMEM((groups, CW, rows), bf16),
            pltpu.VMEM((groups, CW, Q), f32),
            pltpu.VMEM((groups, HG, rows), f32),
            pltpu.VMEM((groups, HG, rows), f32),
            pltpu.VMEM((groups, blocks, GW, N), bf16),
            pltpu.VMEM((groups, GW, N), f32),
            pltpu.VMEM((groups, HG, Q), f32),
            pltpu.VMEM((groups, GW, N), f32),
            pltpu.VMEM((groups, HG, Q), f32),
            pltpu.VMEM((steps, groups, GW, N), bf16),
            pltpu.VMEM((steps, groups, HG, Q), f32),
            pltpu.VMEM((steps, groups, GW, N), bf16),
            pltpu.VMEM((steps, groups, HG, Q), f32),
            pltpu.SemaphoreType.DMA((steps, 2)),
            pltpu.SemaphoreType.DMA((steps, 2)),
        ],
        compiler_params=pltpu.CompilerParams(
            collective_id=1, has_side_effects=True, vmem_limit_bytes=56 * 2**20
        ),
    )(conv, dt, rim, par, heads, skip)


def finish_kernel(part_ref, c_ref, dec_ref, in_ref, gain_ref, out_ref):
    across = jnp.dot(in_ref[0], c_ref[0], preferred_element_type=jnp.float32)
    dec = dec_ref[0]
    grown = across.reshape(HG, P_SIZE, Q) * dec[:, None, :]
    activity = part_ref[0] + grown.reshape(GW, Q)
    square = jnp.sum(activity * activity, axis=0, keepdims=True) * (1.0 / GW)
    normed = (activity * lax.rsqrt(square + epsilon)).T
    out_ref[...] = (normed * gain_ref[0]).astype(jnp.bfloat16)


def finish(part, c, dec, incoming, gain):
    groups, _, rows = part.shape

    def block(tall, wide=Q):
        return pl.BlockSpec((1, tall, wide), lambda g, q: (g, 0, q))

    return pl.pallas_call(
        finish_kernel,
        grid=(groups, rows // Q),
        out_shape=jax.ShapeDtypeStruct((rows, groups * GW), jnp.bfloat16),
        in_specs=[
            block(GW),
            block(N),
            block(HG),
            pl.BlockSpec((1, GW, N), lambda g, q: (g, 0, 0)),
            pl.BlockSpec((1, 1, GW), lambda g, q: (g, 0, 0)),
        ],
        out_specs=pl.BlockSpec((Q, GW), lambda g, q: (q, g)),
        compiler_params=pltpu.CompilerParams(vmem_limit_bytes=32 * 2**20),
    )(part, c, dec, incoming, gain[:, None, :])


def shifted(block, axis, distance):
    devices = range(lax.axis_size(axis))
    route = [(i - distance, i) for i in devices if i - distance in devices]
    return lax.ppermute(block, axis, route)


def per_device(tokens, w_in, conv_w, conv_b, dt_bias, a_log, d_skip, norm_gain):
    lines, ranks = lax.axis_size("chan"), lax.axis_size("seq")
    conv, dt, rim = project(tokens, jnp.swapaxes(w_in, 1, 2), lines, ranks)
    par = jnp.swapaxes(jnp.concatenate([conv_w, conv_b[:, None]], axis=1), 1, 2)
    heads = jnp.stack([dt_bias, a_log], axis=2)
    part, c, dec, incoming = mix(conv, dt, shifted(rim, "seq", 1), par, heads, d_skip, ranks)
    return finish(part, c, dec, incoming, norm_gain)


def solution(mesh):
    return jax.shard_map(
        per_device,
        mesh=mesh,
        in_specs=(
            P("seq", "chan"),
            P("chan", "seq", None),
            P("chan", None, None),
            P("chan", None),
            P("chan", None),
            P("chan", None),
            P("chan", None),
            P("chan", None),
        ),
        out_specs=P("seq", "chan"),
        check_vma=False,
    )
```

```python
import functools
import jax
import jax.numpy as jnp
from jax import lax
from jax.experimental import pallas as pl
from jax.experimental.pallas import tpu as pltpu
from jax.sharding import PartitionSpec as P

P_SIZE = 64
N = 128
KCONV = 4
Q = 128
HG = 16
GW = 1024
CW = 1280
RIM = 16
MESH = pl.DeviceIdType.MESH

epsilon = 1e-05


def project_kernel(
    lines, tok_ref, w_ref, conv_ref, dt_ref, rim_ref,
    tok_all, w_all, acc, own_sem, tok_send, tok_recv, w_own, w_fwd, w_sib, w_recv,
):
    s = lax.axis_index("seq")
    c = lax.axis_index("chan")
    groups, cols, depth = w_ref.shape
    rows, feats = tok_ref.shape
    half = rows // 2
    ratio = feats // depth
    core = s % 2
    sib = s + 1 - 2 * core
    xs = s + 2 - 4 * ((s // 2) % 2)
    ys = s + 4 - 8 * ((s // 4) % 2)
    diag = xs + ys - s
    fwd_shard = xs * (1 - core) + ys * core
    fwd_to = ys * (1 - core) + xs * core

    barrier = pltpu.get_barrier_semaphore()
    for other in (sib, xs, ys):
        pl.semaphore_signal(barrier, inc=1, device_id={"seq": other}, device_id_type=MESH)

    @pl.when(c > 0)
    def _():
        pl.semaphore_signal(barrier, inc=1, device_id={"chan": c - 1}, device_id_type=MESH)

    @pl.when(c < lines - 1)
    def _():
        pl.semaphore_signal(barrier, inc=1, device_id={"chan": c + 1}, device_id_type=MESH)

    pl.semaphore_wait(barrier, 3 + jnp.minimum(c, 1) + jnp.minimum(lines - 1 - c, 1))

    def tok_copy(shard, part, way, own):
        window = pl.ds(part * half, half)
        src = tok_ref.at[window] if own else tok_all.at[shard, window]
        return pltpu.make_async_remote_copy(
            src_ref=src,
            dst_ref=tok_all.at[shard, window],
            send_sem=tok_send.at[way, shard, part],
            recv_sem=tok_recv.at[shard, part],
            device_id={"chan": c + (1 if way else -1)},
            device_id_type=MESH,
        )

    def w_copy(shard, g, sem, to, own):
        src = w_ref.at[g] if own else w_all.at[shard, g]
        return pltpu.make_async_remote_copy(
            src_ref=src,
            dst_ref=w_all.at[shard, g],
            send_sem=sem,
            recv_sem=w_recv.at[shard, g],
            device_id={"seq": to},
            device_id_type=MESH,
        )

    def tok_sends(k, part, act):
        @pl.when((c - k >= 0) & (c < lines - 1))
        def _():
            act(tok_copy(c - k, part, 1, k == 0))

        @pl.when((c + k < lines) & (c > 0))
        def _():
            act(tok_copy(c + k, part, 0, k == 0))

    def tok_arrive(k, part):
        @pl.when(c - k >= 0)
        def _():
            tok_copy(c - k, part, 1, False).wait_recv()

        @pl.when(c + k < lines)
        def _():
            tok_copy(c + k, part, 0, False).wait_recv()

    def start(copy):
        copy.start()

    def sent(copy):
        copy.wait_send()

    own_tok = pltpu.make_async_copy(tok_ref, tok_all.at[c], own_sem.at[0])
    own_w = pltpu.make_async_copy(w_ref, w_all.at[s], own_sem.at[1])
    for part in range(2):
        tok_sends(0, part, start)
        for i, to in enumerate((xs, ys, sib)):
            w_copy(s, part, w_own.at[i, part], to, True).start()
    own_tok.start()
    own_w.start()

    def near_weights(g):
        w_copy(xs, g, w_sib.at[0, g], sib, False).wait_recv()
        w_copy(ys, g, w_sib.at[1, g], sib, False).wait_recv()
        w_copy(fwd_shard, g, w_fwd.at[g], fwd_to, False).start()
        w_copy(xs, g, w_sib.at[0, g], sib, False).start()
        w_copy(ys, g, w_sib.at[1, g], sib, False).start()

    def far_weights(g):
        w_copy(diag, g, w_sib.at[2, g], sib, False).wait_recv()
        w_copy(diag, g, w_sib.at[2, g], sib, False).start()

    def relay(k, part):
        tok_arrive(k, part)
        if k < lines - 1:
            tok_sends(k, part, start)

    acc[...] = jnp.zeros_like(acc)
    tiles = 3
    tall = cols // tiles

    def product(shard, first, last):
        @pl.loop(first * groups * tiles, last * groups * tiles)
        def _(step):
            part = step // (groups * tiles)
            g = (step // tiles) % groups
            window = pl.ds(pl.multiple_of((step % tiles) * tall, 16), tall)
            span = pl.ds(pl.multiple_of(part * half, 128), half)
            total = None
            for i in range(ratio):
                term = lax.dot_general(
                    w_all[shard * ratio + i, g, window, :],
                    tok_all[shard, span, i * depth : (i + 1) * depth],
                    (((1,), (1,)), ((), ())),
                    preferred_element_type=jnp.float32,
                )
                total = term if total is None else total + term
            acc[g, window, span] += total

    relay(1, 0)
    near_weights(0)
    relay(1, 1)
    relay(2, 0)
    near_weights(1)
    relay(2, 1)
    for shard in (sib, sib + xs - s, sib + ys - s):
        for g in range(groups):
            w_copy(shard, g, w_own.at[2, g], sib, False).wait_recv()
    own_tok.wait()
    own_w.wait()
    far = diag // ratio

    @pl.loop(0, lines)
    def _(shard):
        @pl.when((shard != far) & (shard - c < 3) & (c - shard < 3))
        def _():
            product(shard, 0, 2)

    far_weights(0)
    far_weights(1)
    for g in range(groups):
        w_copy(sib + diag - s, g, w_own.at[2, g], sib, False).wait_recv()

    @pl.when((far - c < 3) & (c - far < 3))
    def _():
        product(far, 0, 2)

    for part in range(2):
        tok_arrive(3, part)

        @pl.when(c == 0)
        def _():
            product(3, part, part + 1)

        @pl.when(c == 3)
        def _():
            product(0, part, part + 1)

    for g in range(groups):
        conv_ref[g] = acc[g, :CW, :].astype(jnp.bfloat16)
        dt_ref[g] = acc[g, CW:, :]
        rim_ref[g] = acc[g, :CW, rows - Q :].T[Q - RIM :].astype(jnp.bfloat16)

    for part in range(2):
        for k in range(lines - 1):
            tok_sends(k, part, sent)
        for i, to in enumerate((xs, ys, sib)):
            w_copy(s, part, w_own.at[i, part], to, True).wait_send()
        w_copy(fwd_shard, part, w_fwd.at[part], fwd_to, False).wait_send()
        w_copy(xs, part, w_sib.at[0, part], sib, False).wait_send()
        w_copy(ys, part, w_sib.at[1, part], sib, False).wait_send()
        w_copy(diag, part, w_sib.at[2, part], sib, False).wait_send()


def project(tokens, w_turned, lines, ranks):
    groups, cols, depth = w_turned.shape
    rows, feats = tokens.shape
    shapes = (
        jax.ShapeDtypeStruct((groups, CW, rows), jnp.bfloat16),
        jax.ShapeDtypeStruct((groups, cols - CW, rows), jnp.float32),
        jax.ShapeDtypeStruct((groups, RIM, CW), jnp.bfloat16),
    )
    if ranks == 8 and groups == 2 and lines == 4:
        dma = pltpu.SemaphoreType.DMA
        return pl.pallas_call(
            functools.partial(project_kernel, lines),
            out_shape=shapes,
            in_specs=[pl.BlockSpec(memory_space=pl.ANY)] * 2,
            out_specs=(pl.BlockSpec(memory_space=pltpu.VMEM),) * 3,
            scratch_shapes=[
                pltpu.VMEM((lines, rows, feats), jnp.bfloat16),
                pltpu.VMEM((ranks, groups, cols, depth), jnp.bfloat16),
                pltpu.VMEM((groups, cols, rows), jnp.float32),
                dma((2,)),
                dma((2, lines, 2)),
                dma((lines, 2)),
                dma((3, 2)),
                dma((2,)),
                dma((3, 2)),
                dma((ranks, 2)),
            ],
            compiler_params=pltpu.CompilerParams(
                collective_id=0, has_side_effects=True, vmem_limit_bytes=56 * 2**20
            ),
        )(tokens, w_turned)
    gathered = lax.all_gather(tokens, "chan", axis=1, tiled=True)
    whole = lax.all_gather(w_turned, "seq", axis=2, tiled=True)
    turned = jnp.einsum("gcd,td->gct", whole, gathered, preferred_element_type=jnp.float32)
    conv = turned[:, :CW].astype(jnp.bfloat16)
    return conv, turned[:, CW:], jnp.swapaxes(conv[:, :, rows - RIM :], 1, 2)


def mix_kernel(
    ranks, conv_ref, dt_ref, rim_ref, tap_ref, shift_ref, head_ref, skip_ref,
    part_out, c_out, dec_out, in_out,
    part_ref, dec_ref, in_ref, out_sem, unit_sem, par_ref,
    act, rim_t, dts, cums, states, total, keep, before, keep_before,
    out_state, out_keep, got_state, got_keep, send_sem, recv_sem,
):
    s = lax.axis_index("seq")
    groups, _, rows = conv_ref.shape
    blocks = rows // Q
    steps = ranks.bit_length() - 1
    partners = [s + 2**i - 2 ** (i + 1) * ((s // 2**i) % 2) for i in range(steps)]

    barrier = pltpu.get_barrier_semaphore()
    for other in partners:
        pl.semaphore_signal(barrier, inc=1, device_id={"seq": other}, device_id_type=MESH)
    pl.semaphore_wait(barrier, steps)

    lane = lax.broadcasted_iota(jnp.int32, (32, Q), 1)
    for g in range(groups):
        turned = jnp.concatenate(
            [jnp.zeros((Q - RIM, CW), jnp.float32), rim_ref[g].astype(jnp.float32)], axis=0
        )
        rim_t[g] = turned.T
        taps = jnp.concatenate(
            [tap_ref[g], shift_ref[g : g + 1], jnp.zeros((Q - KCONV - 1, CW), jnp.float32)], axis=0
        )
        par_ref[g] = taps.T

    strips = CW // 32

    @pl.loop(0, groups * strips)
    def _(step):
        g = step // strips
        window = pl.ds(pl.multiple_of((step % strips) * 32, 32), 32)
        par = par_ref[g, window, :]
        taps = [jnp.broadcast_to(par[:, k : k + 1], (32, Q)) for k in range(KCONV + 1)]
        earlier = rim_t[g, window, :]
        old = [pltpu.roll(earlier, d, 1) for d in range(1, KCONV)]
        for q in range(blocks):
            now = conv_ref[g, window, q * Q : (q + 1) * Q].astype(jnp.float32)
            pre = taps[KCONV] + taps[KCONV - 1] * now
            fresh = [pltpu.roll(now, d, 1) for d in range(1, KCONV)]
            for d in range(1, KCONV):
                pre = pre + taps[KCONV - 1 - d] * jnp.where(lane < d, old[d - 1], fresh[d - 1])
            old = fresh
            value = 0.5 * pre * (1.0 + jnp.tanh(0.5 * pre))
            act[g, window, q * Q : (q + 1) * Q] = value.astype(jnp.bfloat16)

    row = lax.broadcasted_iota(jnp.int32, (Q, Q), 0)
    col = lax.broadcasted_iota(jnp.int32, (Q, Q), 1)
    causal = row <= col
    upper = jnp.where(causal, 1.0, 0.0)
    for g in range(groups):
        heads = head_ref[g]
        raw = dt_ref[g] + heads[:, 0:1]
        step_dt = jnp.maximum(raw, 0.0) + jnp.log1p(jnp.exp(-jnp.abs(raw)))
        dts[g] = step_dt
        slope = -jnp.exp(heads[:, 1:2]) * step_dt
        base = jnp.zeros((HG, 1), jnp.float32)
        for q in range(blocks):
            tile = slice(q * Q, (q + 1) * Q)
            cum = jnp.dot(
                slope[:, tile], upper,
                precision=lax.Precision.HIGHEST, preferred_element_type=jnp.float32,
            )
            cums[g, :, tile] = cum
            dec_ref[g, :, tile] = jnp.exp(cum + base)
            base = base + cum[:, Q - 1 :]
        keep[g] = jnp.broadcast_to(jnp.exp(base), (HG, Q))
        total[g] = jnp.zeros((GW, N), jnp.float32)

    early = [
        pltpu.make_async_copy(act.at[:, pl.ds(GW + N, N)], c_out, out_sem.at[0]),
        pltpu.make_async_copy(dec_ref, dec_out, out_sem.at[1]),
    ]
    for copy in early:
        copy.start()

    @pl.loop(0, groups * blocks)
    def _(unit):
        g, q = unit // blocks, unit % blocks
        tile = pl.ds(pl.multiple_of(q * Q, Q), Q)
        cum = cums[g, :, tile]
        last = cum[:, Q - 1 :]
        tail = jnp.exp(last - cum) * dts[g, :, tile]
        held = jnp.broadcast_to(jnp.exp(last), (HG, Q))
        states[g, q] = total[g].astype(jnp.bfloat16)
        b = act[g, GW : GW + N, tile].astype(jnp.float32).T.astype(jnp.bfloat16)
        for h in range(0, HG, 4):
            x = act[g, h * P_SIZE : (h + 4) * P_SIZE, tile].astype(jnp.float32)
            scaled = x.reshape(4, P_SIZE, Q) * tail[h : h + 4][:, None, :]
            scaled = scaled.reshape(4 * P_SIZE, Q).astype(jnp.bfloat16)
            fresh = jnp.dot(scaled, b, preferred_element_type=jnp.float32)
            for i in range(4):
                span = slice((h + i) * P_SIZE, (h + i + 1) * P_SIZE)
                total[g, span, :] = (
                    held[h + i : h + i + 1] * total[g, span, :]
                    + fresh[i * P_SIZE : (i + 1) * P_SIZE]
                )

    def leave(unit):
        g, q = unit // blocks, unit % blocks
        tile = pl.ds(pl.multiple_of(q * Q, Q), Q)
        return pltpu.make_async_copy(
            part_ref.at[g, :, tile], part_out.at[g, :, tile], unit_sem.at[unit]
        )

    def inner(unit):
        g, q = unit // blocks, unit % blocks
        tile = pl.ds(pl.multiple_of(q * Q, Q), Q)
        cum = cums[g, :, tile]
        tall = jnp.concatenate([cum, jnp.zeros((Q - HG, Q), jnp.float32)], axis=0).T
        dt = dts[g, :, tile]
        grown = jnp.exp(cum)
        b = act[g, GW : GW + N, tile].astype(jnp.float32).T.astype(jnp.bfloat16)
        c = act[g, GW + N :, tile]
        scores = jnp.where(causal, jnp.dot(b, c, preferred_element_type=jnp.float32), 0.0)
        for h in range(HG):
            span = slice(h * P_SIZE, (h + 1) * P_SIZE)
            x = act[g, span, tile].astype(jnp.float32)
            if h % 4 == 0:
                wide = slice(h * P_SIZE, (h + 4) * P_SIZE)
                four = jnp.dot(states[g, q, wide, :], c, preferred_element_type=jnp.float32)
            across = four[(h % 4) * P_SIZE : (h % 4 + 1) * P_SIZE]
            spread = cum[h : h + 1] - tall[:, h : h + 1]
            weights = (scores * jnp.exp(jnp.minimum(spread, 0.0))).astype(jnp.bfloat16)
            stepped = (x * dt[h : h + 1]).astype(jnp.bfloat16)
            y = jnp.dot(stepped, weights, preferred_element_type=jnp.float32)
            part_ref[g, span, tile] = y + grown[h : h + 1] * across + skip_ref[g, h] * x
        leave(unit).start()

    def exchange(i):
        return [
            pltpu.make_async_remote_copy(
                src_ref=src.at[i], dst_ref=dst.at[i],
                send_sem=send_sem.at[i, j], recv_sem=recv_sem.at[i, j],
                device_id={"seq": partners[i]}, device_id_type=MESH,
            )
            for j, (src, dst) in enumerate(((out_state, got_state), (out_keep, got_keep)))
        ]

    def send(i):
        out_state[i] = total[...].astype(jnp.bfloat16)
        out_keep[i] = keep[...]
        for copy in exchange(i):
            copy.start()

    before[...] = jnp.zeros_like(before)
    keep_before[...] = jnp.ones_like(keep_before)
    units = groups * blocks
    for i in range(steps):
        send(i)
        pl.loop(units * i // steps, units * (i + 1) // steps)(inner)
        for copy in exchange(i):
            copy.wait_recv()
        upper_half = (s // 2**i) % 2

        @pl.when(upper_half == 1)
        def _():
            for g in range(groups):
                for h in range(HG):
                    span = slice(h * P_SIZE, (h + 1) * P_SIZE)
                    got = got_state[i, g, span, :].astype(jnp.float32)
                    before[g, span, :] += keep_before[g, h : h + 1] * got
                    if i < steps - 1:
                        total[g, span, :] += keep[g, h : h + 1] * got
            keep_before[...] = keep_before[...] * got_keep[i]

        if i < steps - 1:

            @pl.when(upper_half == 0)
            def _():
                for g in range(groups):
                    for h in range(HG):
                        span = slice(h * P_SIZE, (h + 1) * P_SIZE)
                        got = got_state[i, g, span, :].astype(jnp.float32)
                        total[g, span, :] = got_keep[i, g, h : h + 1] * total[g, span, :] + got

            keep[...] = keep[...] * got_keep[i]

    in_ref[...] = before[...].astype(jnp.bfloat16)
    late = pltpu.make_async_copy(in_ref, in_out, out_sem.at[2])
    late.start()
    for copy in early:
        copy.wait()

    @pl.loop(0, units)
    def _(unit):
        leave(unit).wait()

    late.wait()
    for i in range(steps):
        for copy in exchange(i):
            copy.wait_send()


def mix(conv, dt, rim, taps, shift, heads, skip, ranks):
    groups, _, rows = conv.shape
    blocks = rows // Q
    steps = ranks.bit_length() - 1
    vmem = pl.BlockSpec(memory_space=pltpu.VMEM)
    f32, bf16 = jnp.float32, jnp.bfloat16
    return pl.pallas_call(
        functools.partial(mix_kernel, ranks),
        out_shape=(
            jax.ShapeDtypeStruct((groups, GW, rows), f32),
            jax.ShapeDtypeStruct((groups, N, rows), bf16),
            jax.ShapeDtypeStruct((groups, HG, rows), f32),
            jax.ShapeDtypeStruct((groups, GW, N), bf16),
        ),
        in_specs=[vmem] * 6 + [pl.BlockSpec(memory_space=pltpu.SMEM)],
        out_specs=(pl.BlockSpec(memory_space=pl.ANY),) * 4,
        scratch_shapes=[
            pltpu.VMEM((groups, GW, rows), f32),
            pltpu.VMEM((groups, HG, rows), f32),
            pltpu.VMEM((groups, GW, N), bf16),
            pltpu.SemaphoreType.DMA((3,)),
            pltpu.SemaphoreType.DMA((groups * blocks,)),
            pltpu.VMEM((groups, CW, Q), f32),
            pltpu.VMEM((groups, CW, rows), bf16),
            pltpu.VMEM((groups, CW, Q), f32),
            pltpu.VMEM((groups, HG, rows), f32),
            pltpu.VMEM((groups, HG, rows), f32),
            pltpu.VMEM((groups, blocks, GW, N), bf16),
            pltpu.VMEM((groups, GW, N), f32),
            pltpu.VMEM((groups, HG, Q), f32),
            pltpu.VMEM((groups, GW, N), f32),
            pltpu.VMEM((groups, HG, Q), f32),
            pltpu.VMEM((steps, groups, GW, N), bf16),
            pltpu.VMEM((steps, groups, HG, Q), f32),
            pltpu.VMEM((steps, groups, GW, N), bf16),
            pltpu.VMEM((steps, groups, HG, Q), f32),
            pltpu.SemaphoreType.DMA((steps, 2)),
            pltpu.SemaphoreType.DMA((steps, 2)),
        ],
        compiler_params=pltpu.CompilerParams(
            collective_id=1, has_side_effects=True, vmem_limit_bytes=56 * 2**20
        ),
    )(conv, dt, rim, taps, shift, heads, skip)


def finish_kernel(part_ref, c_ref, dec_ref, in_ref, gain_ref, out_ref):
    across = jnp.dot(in_ref[0], c_ref[0], preferred_element_type=jnp.float32)
    dec = dec_ref[0]
    grown = across.reshape(HG, P_SIZE, Q) * dec[:, None, :]
    activity = part_ref[0] + grown.reshape(GW, Q)
    square = jnp.sum(activity * activity, axis=0, keepdims=True) * (1.0 / GW)
    normed = (activity * lax.rsqrt(square + epsilon)).T
    out_ref[...] = (normed * gain_ref[0]).astype(jnp.bfloat16)


def finish(part, c, dec, incoming, gain):
    groups, _, rows = part.shape

    def block(tall, wide=Q):
        return pl.BlockSpec((1, tall, wide), lambda g, q: (g, 0, q))

    return pl.pallas_call(
        finish_kernel,
        grid=(groups, rows // Q),
        out_shape=jax.ShapeDtypeStruct((rows, groups * GW), jnp.bfloat16),
        in_specs=[
            block(GW),
            block(N),
            block(HG),
            pl.BlockSpec((1, GW, N), lambda g, q: (g, 0, 0)),
            pl.BlockSpec((1, 1, GW), lambda g, q: (g, 0, 0)),
        ],
        out_specs=pl.BlockSpec((Q, GW), lambda g, q: (q, g)),
        compiler_params=pltpu.CompilerParams(vmem_limit_bytes=32 * 2**20),
    )(part, c, dec, incoming, gain[:, None, :])


def shifted(block, axis, distance):
    devices = range(lax.axis_size(axis))
    route = [(i - distance, i) for i in devices if i - distance in devices]
    return lax.ppermute(block, axis, route)


def per_device(tokens, w_in, conv_w, conv_b, dt_bias, a_log, d_skip, norm_gain):
    lines, ranks = lax.axis_size("chan"), lax.axis_size("seq")
    conv, dt, rim = project(tokens, jnp.swapaxes(w_in, 1, 2), lines, ranks)
    heads = jnp.stack([dt_bias, a_log], axis=2)
    rim = shifted(rim, "seq", 1)
    part, c, dec, incoming = mix(conv, dt, rim, conv_w, conv_b, heads, d_skip, ranks)
    return finish(part, c, dec, incoming, norm_gain)


def solution(mesh):
    return jax.shard_map(
        per_device,
        mesh=mesh,
        in_specs=(
            P("seq", "chan"),
            P("chan", "seq", None),
            P("chan", None, None),
            P("chan", None),
            P("chan", None),
            P("chan", None),
            P("chan", None),
            P("chan", None),
        ),
        out_specs=P("seq", "chan"),
        check_vma=False,
    )
```

```python
import functools
import jax
import jax.numpy as jnp
from jax import lax
from jax.experimental import pallas as pl
from jax.experimental.pallas import tpu as pltpu
from jax.sharding import PartitionSpec as P

P_SIZE = 64
N = 128
KCONV = 4
Q = 128
HG = 16
GW = 1024
CW = 1280
RIM = 16
MESH = pl.DeviceIdType.MESH

epsilon = 1e-05
LOG2_E = 1.4426950408889634


def project_kernel(
    lines, tok_ref, w_ref, conv_ref, dt_ref, rim_ref,
    tok_all, w_all, acc, own_sem, tok_send, tok_recv, w_own, w_fwd, w_sib, w_recv,
):
    s = lax.axis_index("seq")
    c = lax.axis_index("chan")
    groups, cols, depth = w_ref.shape
    rows, feats = tok_ref.shape
    half = rows // 2
    ratio = feats // depth
    core = s % 2
    sib = s + 1 - 2 * core
    xs = s + 2 - 4 * ((s // 2) % 2)
    ys = s + 4 - 8 * ((s // 4) % 2)
    diag = xs + ys - s
    fwd_shard = xs * (1 - core) + ys * core
    fwd_to = ys * (1 - core) + xs * core

    barrier = pltpu.get_barrier_semaphore()
    for other in (sib, xs, ys):
        pl.semaphore_signal(barrier, inc=1, device_id={"seq": other}, device_id_type=MESH)

    @pl.when(c > 0)
    def _():
        pl.semaphore_signal(barrier, inc=1, device_id={"chan": c - 1}, device_id_type=MESH)

    @pl.when(c < lines - 1)
    def _():
        pl.semaphore_signal(barrier, inc=1, device_id={"chan": c + 1}, device_id_type=MESH)

    pl.semaphore_wait(barrier, 3 + jnp.minimum(c, 1) + jnp.minimum(lines - 1 - c, 1))

    def tok_copy(shard, part, way, own):
        window = pl.ds(part * half, half)
        src = tok_ref.at[window] if own else tok_all.at[shard, window]
        return pltpu.make_async_remote_copy(
            src_ref=src,
            dst_ref=tok_all.at[shard, window],
            send_sem=tok_send.at[way, shard, part],
            recv_sem=tok_recv.at[shard, part],
            device_id={"chan": c + (1 if way else -1)},
            device_id_type=MESH,
        )

    def w_copy(shard, g, sem, to, own):
        src = w_ref.at[g] if own else w_all.at[shard, g]
        return pltpu.make_async_remote_copy(
            src_ref=src,
            dst_ref=w_all.at[shard, g],
            send_sem=sem,
            recv_sem=w_recv.at[shard, g],
            device_id={"seq": to},
            device_id_type=MESH,
        )

    def tok_sends(k, part, act):
        @pl.when((c - k >= 0) & (c < lines - 1))
        def _():
            act(tok_copy(c - k, part, 1, k == 0))

        @pl.when((c + k < lines) & (c > 0))
        def _():
            act(tok_copy(c + k, part, 0, k == 0))

    def tok_arrive(k, part):
        @pl.when(c - k >= 0)
        def _():
            tok_copy(c - k, part, 1, False).wait_recv()

        @pl.when(c + k < lines)
        def _():
            tok_copy(c + k, part, 0, False).wait_recv()

    def start(copy):
        copy.start()

    def sent(copy):
        copy.wait_send()

    own_tok = pltpu.make_async_copy(tok_ref, tok_all.at[c], own_sem.at[0])
    own_w = pltpu.make_async_copy(w_ref, w_all.at[s], own_sem.at[1])
    for part in range(2):
        tok_sends(0, part, start)
        for i, to in enumerate((xs, ys, sib)):
            w_copy(s, part, w_own.at[i, part], to, True).start()
    own_tok.start()
    own_w.start()

    def near_weights(g):
        w_copy(xs, g, w_sib.at[0, g], sib, False).wait_recv()
        w_copy(ys, g, w_sib.at[1, g], sib, False).wait_recv()
        w_copy(fwd_shard, g, w_fwd.at[g], fwd_to, False).start()
        w_copy(xs, g, w_sib.at[0, g], sib, False).start()
        w_copy(ys, g, w_sib.at[1, g], sib, False).start()

    def far_weights(g):
        w_copy(diag, g, w_sib.at[2, g], sib, False).wait_recv()
        w_copy(diag, g, w_sib.at[2, g], sib, False).start()

    def relay(k, part):
        tok_arrive(k, part)
        if k < lines - 1:
            tok_sends(k, part, start)

    acc[...] = jnp.zeros_like(acc)
    tiles = 3
    tall = cols // tiles

    def product(shard, first, last):
        @pl.loop(first * groups * tiles, last * groups * tiles)
        def _(step):
            part = step // (groups * tiles)
            g = (step // tiles) % groups
            window = pl.ds(pl.multiple_of((step % tiles) * tall, 16), tall)
            span = pl.ds(pl.multiple_of(part * half, 128), half)
            total = None
            for i in range(ratio):
                term = lax.dot_general(
                    w_all[shard * ratio + i, g, window, :],
                    tok_all[shard, span, i * depth : (i + 1) * depth],
                    (((1,), (1,)), ((), ())),
                    preferred_element_type=jnp.float32,
                )
                total = term if total is None else total + term
            acc[g, window, span] += total

    relay(1, 0)
    near_weights(0)
    relay(1, 1)
    relay(2, 0)
    near_weights(1)
    relay(2, 1)
    for shard in (sib, sib + xs - s, sib + ys - s):
        for g in range(groups):
            w_copy(shard, g, w_own.at[2, g], sib, False).wait_recv()
    own_tok.wait()
    own_w.wait()
    far = diag // ratio

    @pl.loop(0, lines)
    def _(shard):
        @pl.when((shard != far) & (shard - c < 3) & (c - shard < 3))
        def _():
            product(shard, 0, 2)

    far_weights(0)
    far_weights(1)
    for g in range(groups):
        w_copy(sib + diag - s, g, w_own.at[2, g], sib, False).wait_recv()

    @pl.when((far - c < 3) & (c - far < 3))
    def _():
        product(far, 0, 2)

    for part in range(2):
        tok_arrive(3, part)

        @pl.when(c == 0)
        def _():
            product(3, part, part + 1)

        @pl.when(c == 3)
        def _():
            product(0, part, part + 1)

    for g in range(groups):
        conv_ref[g] = acc[g, :CW, :].astype(jnp.bfloat16)
        dt_ref[g] = acc[g, CW:, :]
        rim_ref[g] = acc[g, :CW, rows - Q :].T[Q - RIM :].astype(jnp.bfloat16)

    for part in range(2):
        for k in range(lines - 1):
            tok_sends(k, part, sent)
        for i, to in enumerate((xs, ys, sib)):
            w_copy(s, part, w_own.at[i, part], to, True).wait_send()
        w_copy(fwd_shard, part, w_fwd.at[part], fwd_to, False).wait_send()
        w_copy(xs, part, w_sib.at[0, part], sib, False).wait_send()
        w_copy(ys, part, w_sib.at[1, part], sib, False).wait_send()
        w_copy(diag, part, w_sib.at[2, part], sib, False).wait_send()


def project(tokens, w_turned, lines, ranks):
    groups, cols, depth = w_turned.shape
    rows, feats = tokens.shape
    shapes = (
        jax.ShapeDtypeStruct((groups, CW, rows), jnp.bfloat16),
        jax.ShapeDtypeStruct((groups, cols - CW, rows), jnp.float32),
        jax.ShapeDtypeStruct((groups, RIM, CW), jnp.bfloat16),
    )
    if ranks == 8 and groups == 2 and lines == 4:
        dma = pltpu.SemaphoreType.DMA
        return pl.pallas_call(
            functools.partial(project_kernel, lines),
            out_shape=shapes,
            in_specs=[pl.BlockSpec(memory_space=pl.ANY)] * 2,
            out_specs=(pl.BlockSpec(memory_space=pltpu.VMEM),) * 3,
            scratch_shapes=[
                pltpu.VMEM((lines, rows, feats), jnp.bfloat16),
                pltpu.VMEM((ranks, groups, cols, depth), jnp.bfloat16),
                pltpu.VMEM((groups, cols, rows), jnp.float32),
                dma((2,)),
                dma((2, lines, 2)),
                dma((lines, 2)),
                dma((3, 2)),
                dma((2,)),
                dma((3, 2)),
                dma((ranks, 2)),
            ],
            compiler_params=pltpu.CompilerParams(
                collective_id=0, has_side_effects=True, vmem_limit_bytes=56 * 2**20
            ),
        )(tokens, w_turned)
    gathered = lax.all_gather(tokens, "chan", axis=1, tiled=True)
    whole = lax.all_gather(w_turned, "seq", axis=2, tiled=True)
    turned = jnp.einsum("gcd,td->gct", whole, gathered, preferred_element_type=jnp.float32)
    conv = turned[:, :CW].astype(jnp.bfloat16)
    return conv, turned[:, CW:], jnp.swapaxes(conv[:, :, rows - RIM :], 1, 2)


def mix_kernel(
    ranks, conv_ref, dt_ref, rim_ref, tap_ref, shift_ref, head_ref, skip_ref,
    part_out, c_out, dec_out, in_out,
    part_ref, dec_ref, in_ref, out_sem, unit_sem, par_ref,
    act, rim_t, dts, cums, states, total, keep, before, keep_before,
    out_state, out_keep, got_state, got_keep, send_sem, recv_sem,
):
    s = lax.axis_index("seq")
    groups, _, rows = conv_ref.shape
    blocks = rows // Q
    steps = ranks.bit_length() - 1
    partners = [s + 2**i - 2 ** (i + 1) * ((s // 2**i) % 2) for i in range(steps)]

    barrier = pltpu.get_barrier_semaphore()
    for other in partners:
        pl.semaphore_signal(barrier, inc=1, device_id={"seq": other}, device_id_type=MESH)
    pl.semaphore_wait(barrier, steps)

    lane = lax.broadcasted_iota(jnp.int32, (32, Q), 1)
    for g in range(groups):
        turned = jnp.concatenate(
            [jnp.zeros((Q - RIM, CW), jnp.float32), rim_ref[g].astype(jnp.float32)], axis=0
        )
        rim_t[g] = turned.T
        taps = jnp.concatenate(
            [tap_ref[g], shift_ref[g : g + 1], jnp.zeros((Q - KCONV - 1, CW), jnp.float32)], axis=0
        )
        par_ref[g] = taps.T

    strips = CW // 32

    @pl.loop(0, groups * strips)
    def _(step):
        g = step // strips
        window = pl.ds(pl.multiple_of((step % strips) * 32, 32), 32)
        par = par_ref[g, window, :]
        taps = [jnp.broadcast_to(par[:, k : k + 1], (32, Q)) for k in range(KCONV + 1)]
        earlier = rim_t[g, window, :]
        old = [pltpu.roll(earlier, d, 1) for d in range(1, KCONV)]
        for q in range(blocks):
            now = conv_ref[g, window, q * Q : (q + 1) * Q].astype(jnp.float32)
            pre = taps[KCONV] + taps[KCONV - 1] * now
            fresh = [pltpu.roll(now, d, 1) for d in range(1, KCONV)]
            for d in range(1, KCONV):
                pre = pre + taps[KCONV - 1 - d] * jnp.where(lane < d, old[d - 1], fresh[d - 1])
            old = fresh
            value = 0.5 * pre * (1.0 + jnp.tanh(0.5 * pre))
            act[g, window, q * Q : (q + 1) * Q] = value.astype(jnp.bfloat16)

    row = lax.broadcasted_iota(jnp.int32, (Q, Q), 0)
    col = lax.broadcasted_iota(jnp.int32, (Q, Q), 1)
    causal = row <= col
    upper = jnp.where(causal, 1.0, 0.0)
    for g in range(groups):
        heads = head_ref[g]
        raw = dt_ref[g] + heads[:, 0:1]
        step_dt = jnp.maximum(raw, 0.0) + jnp.log1p(jnp.exp(-jnp.abs(raw)))
        dts[g] = step_dt
        slope = -jnp.exp(heads[:, 1:2]) * step_dt
        base = jnp.zeros((HG, 1), jnp.float32)
        for q in range(blocks):
            tile = slice(q * Q, (q + 1) * Q)
            cum = jnp.dot(
                slope[:, tile], upper,
                precision=lax.Precision.HIGHEST, preferred_element_type=jnp.float32,
            )
            cums[g, :, tile] = cum
            dec_ref[g, :, tile] = jnp.exp(cum + base)
            base = base + cum[:, Q - 1 :]
        keep[g] = jnp.broadcast_to(jnp.exp(base), (HG, Q))
        total[g] = jnp.zeros((GW, N), jnp.float32)

    early = [
        pltpu.make_async_copy(act.at[:, pl.ds(GW + N, N)], c_out, out_sem.at[0]),
        pltpu.make_async_copy(dec_ref, dec_out, out_sem.at[1]),
    ]
    for copy in early:
        copy.start()

    @pl.loop(0, groups * blocks)
    def _(unit):
        g, q = unit // blocks, unit % blocks
        tile = pl.ds(pl.multiple_of(q * Q, Q), Q)
        cum = cums[g, :, tile]
        last = cum[:, Q - 1 :]
        tail = jnp.exp(last - cum) * dts[g, :, tile]
        held = jnp.broadcast_to(jnp.exp(last), (HG, Q))
        states[g, q] = total[g].astype(jnp.bfloat16)
        b = act[g, GW : GW + N, tile].astype(jnp.float32).T.astype(jnp.bfloat16)
        for h in range(0, HG, 4):
            x = act[g, h * P_SIZE : (h + 4) * P_SIZE, tile].astype(jnp.float32)
            scaled = x.reshape(4, P_SIZE, Q) * tail[h : h + 4][:, None, :]
            scaled = scaled.reshape(4 * P_SIZE, Q).astype(jnp.bfloat16)
            fresh = jnp.dot(scaled, b, preferred_element_type=jnp.float32)
            for i in range(4):
                span = slice((h + i) * P_SIZE, (h + i + 1) * P_SIZE)
                total[g, span, :] = (
                    held[h + i : h + i + 1] * total[g, span, :]
                    + fresh[i * P_SIZE : (i + 1) * P_SIZE]
                )

    def leave(unit):
        g, q = unit // blocks, unit % blocks
        tile = pl.ds(pl.multiple_of(q * Q, Q), Q)
        return pltpu.make_async_copy(
            part_ref.at[g, :, tile], part_out.at[g, :, tile], unit_sem.at[unit]
        )

    def inner(unit):
        g, q = unit // blocks, unit % blocks
        tile = pl.ds(pl.multiple_of(q * Q, Q), Q)
        cum = cums[g, :, tile]
        grown = jnp.exp(cum)
        cum = cum * LOG2_E
        tall = jnp.concatenate([cum, jnp.zeros((Q - HG, Q), jnp.float32)], axis=0).T
        dt = dts[g, :, tile]
        b = act[g, GW : GW + N, tile].astype(jnp.float32).T.astype(jnp.bfloat16)
        c = act[g, GW + N :, tile]
        scores = jnp.where(causal, jnp.dot(b, c, preferred_element_type=jnp.float32), 0.0)
        for h in range(HG):
            span = slice(h * P_SIZE, (h + 1) * P_SIZE)
            x = act[g, span, tile].astype(jnp.float32)
            if h % 4 == 0:
                wide = slice(h * P_SIZE, (h + 4) * P_SIZE)
                four = jnp.dot(states[g, q, wide, :], c, preferred_element_type=jnp.float32)
            across = four[(h % 4) * P_SIZE : (h % 4 + 1) * P_SIZE]
            spread = cum[h : h + 1] - tall[:, h : h + 1]
            weights = (scores * jnp.exp2(jnp.minimum(spread, 0.0))).astype(jnp.bfloat16)
            stepped = (x * dt[h : h + 1]).astype(jnp.bfloat16)
            y = jnp.dot(stepped, weights, preferred_element_type=jnp.float32)
            part_ref[g, span, tile] = y + grown[h : h + 1] * across + skip_ref[g, h] * x
        leave(unit).start()

    def exchange(i):
        return [
            pltpu.make_async_remote_copy(
                src_ref=src.at[i], dst_ref=dst.at[i],
                send_sem=send_sem.at[i, j], recv_sem=recv_sem.at[i, j],
                device_id={"seq": partners[i]}, device_id_type=MESH,
            )
            for j, (src, dst) in enumerate(((out_state, got_state), (out_keep, got_keep)))
        ]

    def send(i):
        out_state[i] = total[...].astype(jnp.bfloat16)
        out_keep[i] = keep[...]
        for copy in exchange(i):
            copy.start()

    before[...] = jnp.zeros_like(before)
    keep_before[...] = jnp.ones_like(keep_before)
    units = groups * blocks
    cuts = [0] + [1 + (units - 1) * i // (steps - 1) for i in range(steps)]
    for i in range(steps):
        send(i)
        pl.loop(cuts[i], cuts[i + 1])(inner)
        for copy in exchange(i):
            copy.wait_recv()
        upper_half = (s // 2**i) % 2

        @pl.when(upper_half == 1)
        def _():
            for g in range(groups):
                for h in range(HG):
                    span = slice(h * P_SIZE, (h + 1) * P_SIZE)
                    got = got_state[i, g, span, :].astype(jnp.float32)
                    before[g, span, :] += keep_before[g, h : h + 1] * got
                    if i < steps - 1:
                        total[g, span, :] += keep[g, h : h + 1] * got
            keep_before[...] = keep_before[...] * got_keep[i]

        if i < steps - 1:

            @pl.when(upper_half == 0)
            def _():
                for g in range(groups):
                    for h in range(HG):
                        span = slice(h * P_SIZE, (h + 1) * P_SIZE)
                        got = got_state[i, g, span, :].astype(jnp.float32)
                        total[g, span, :] = got_keep[i, g, h : h + 1] * total[g, span, :] + got

            keep[...] = keep[...] * got_keep[i]

    in_ref[...] = before[...].astype(jnp.bfloat16)
    late = pltpu.make_async_copy(in_ref, in_out, out_sem.at[2])
    late.start()
    for copy in early:
        copy.wait()

    @pl.loop(0, units)
    def _(unit):
        leave(unit).wait()

    late.wait()
    for i in range(steps):
        for copy in exchange(i):
            copy.wait_send()


def mix(conv, dt, rim, taps, shift, heads, skip, ranks):
    groups, _, rows = conv.shape
    blocks = rows // Q
    steps = ranks.bit_length() - 1
    vmem = pl.BlockSpec(memory_space=pltpu.VMEM)
    f32, bf16 = jnp.float32, jnp.bfloat16
    return pl.pallas_call(
        functools.partial(mix_kernel, ranks),
        out_shape=(
            jax.ShapeDtypeStruct((groups, GW, rows), f32),
            jax.ShapeDtypeStruct((groups, N, rows), bf16),
            jax.ShapeDtypeStruct((groups, HG, rows), f32),
            jax.ShapeDtypeStruct((groups, GW, N), bf16),
        ),
        in_specs=[vmem] * 6 + [pl.BlockSpec(memory_space=pltpu.SMEM)],
        out_specs=(pl.BlockSpec(memory_space=pl.ANY),) * 4,
        scratch_shapes=[
            pltpu.VMEM((groups, GW, rows), f32),
            pltpu.VMEM((groups, HG, rows), f32),
            pltpu.VMEM((groups, GW, N), bf16),
            pltpu.SemaphoreType.DMA((3,)),
            pltpu.SemaphoreType.DMA((groups * blocks,)),
            pltpu.VMEM((groups, CW, Q), f32),
            pltpu.VMEM((groups, CW, rows), bf16),
            pltpu.VMEM((groups, CW, Q), f32),
            pltpu.VMEM((groups, HG, rows), f32),
            pltpu.VMEM((groups, HG, rows), f32),
            pltpu.VMEM((groups, blocks, GW, N), bf16),
            pltpu.VMEM((groups, GW, N), f32),
            pltpu.VMEM((groups, HG, Q), f32),
            pltpu.VMEM((groups, GW, N), f32),
            pltpu.VMEM((groups, HG, Q), f32),
            pltpu.VMEM((steps, groups, GW, N), bf16),
            pltpu.VMEM((steps, groups, HG, Q), f32),
            pltpu.VMEM((steps, groups, GW, N), bf16),
            pltpu.VMEM((steps, groups, HG, Q), f32),
            pltpu.SemaphoreType.DMA((steps, 2)),
            pltpu.SemaphoreType.DMA((steps, 2)),
        ],
        compiler_params=pltpu.CompilerParams(
            collective_id=1, has_side_effects=True, vmem_limit_bytes=56 * 2**20
        ),
    )(conv, dt, rim, taps, shift, heads, skip)


def finish_kernel(part_ref, c_ref, dec_ref, in_ref, gain_ref, out_ref):
    across = jnp.dot(in_ref[0], c_ref[0], preferred_element_type=jnp.float32)
    dec = dec_ref[0]
    grown = across.reshape(HG, P_SIZE, Q) * dec[:, None, :]
    activity = part_ref[0] + grown.reshape(GW, Q)
    square = jnp.sum(activity * activity, axis=0, keepdims=True) * (1.0 / GW)
    normed = (activity * lax.rsqrt(square + epsilon)).T
    out_ref[...] = (normed * gain_ref[0]).astype(jnp.bfloat16)


def finish(part, c, dec, incoming, gain):
    groups, _, rows = part.shape

    def block(tall, wide=Q):
        return pl.BlockSpec((1, tall, wide), lambda g, q: (g, 0, q))

    return pl.pallas_call(
        finish_kernel,
        grid=(groups, rows // Q),
        out_shape=jax.ShapeDtypeStruct((rows, groups * GW), jnp.bfloat16),
        in_specs=[
            block(GW),
            block(N),
            block(HG),
            pl.BlockSpec((1, GW, N), lambda g, q: (g, 0, 0)),
            pl.BlockSpec((1, 1, GW), lambda g, q: (g, 0, 0)),
        ],
        out_specs=pl.BlockSpec((Q, GW), lambda g, q: (q, g)),
        compiler_params=pltpu.CompilerParams(vmem_limit_bytes=60 * 2**20),
    )(part, c, dec, incoming, gain[:, None, :])


def shifted(block, axis, distance):
    devices = range(lax.axis_size(axis))
    route = [(i - distance, i) for i in devices if i - distance in devices]
    return lax.ppermute(block, axis, route)


def per_device(tokens, w_in, conv_w, conv_b, dt_bias, a_log, d_skip, norm_gain):
    lines, ranks = lax.axis_size("chan"), lax.axis_size("seq")
    conv, dt, rim = project(tokens, jnp.swapaxes(w_in, 1, 2), lines, ranks)
    heads = jnp.stack([dt_bias, a_log], axis=2)
    rim = shifted(rim, "seq", 1)
    part, c, dec, incoming = mix(conv, dt, rim, conv_w, conv_b, heads, d_skip, ranks)
    return finish(part, c, dec, incoming, norm_gain)


def solution(mesh):
    return jax.shard_map(
        per_device,
        mesh=mesh,
        in_specs=(
            P("seq", "chan"),
            P("chan", "seq", None),
            P("chan", None, None),
            P("chan", None),
            P("chan", None),
            P("chan", None),
            P("chan", None),
            P("chan", None),
        ),
        out_specs=P("seq", "chan"),
        check_vma=False,
    )
```
